512 devices in a mesh: ctx: 16 (over y, x_hi), head: 32 (over z, x_lo, core).
Axes of the slice: x: 4 (x_hi: 2, x_lo: 2; x = x_hi * 2 + x_lo), y: 8, z: 8, core: 2. Of those that a mesh axis runs over, the one named last changes fastest.
Arguments:
- queries: bfloat16 [512, 12288], P('ctx', 'head'), may hold values from -6 to 6
- cache_keys: bfloat16 [32, 16384, 128], P('head', 'ctx'), may hold values from -6 to 6
- cache_values: bfloat16 [32, 16384, 128], P('head', 'ctx'), may hold values from -6 to 6
- turn_keys: bfloat16 [32, 128, 128], P('head', 'ctx'), may hold values from -12 to 12
- turn_values: bfloat16 [32, 128, 128], P('head', 'ctx'), may hold values from -6 to 6
- cache_fill: int32 [16], P('ctx'), may hold values from 1 to 1024, 8192 in all
- turn_positions: int32 [512], replicated, may hold values from 0 to 511, each once
Outputs:
- attention_out: bfloat16 [512, 12288], P('ctx', 'head')
The draws below stay inside these ranges and needn't reach their ends.
Inputs may be any that keep to these rules, and one draw needn't show every extreme that they name: `turn_positions`: each of 0 to 511 exactly once.
All inputs are finite; a program needn't handle non-finite values. No bound on the sum of `cache_fill` on one device may be relied on, other than what follows from the above.
Results may differ from the reference program's by a relative error of at most 0.005.
Values may be sent and summed in bfloat16 or wider, within the bound.
No kernel may reach another device: no remote copies, remote signals or barrier semaphores. Data moves between devices by JAX's collectives and lax.ppermute only.
A program may use at most 128 MiB of HBM per device.

```python
import math
import jax
import jax.numpy as jnp
import numpy as np
from jax import lax

HEAD_DIM = 128
Q_HEADS = 96
KV_HEADS = 8
SLOTS = 1024
KV_SHARERS = 4
TURN = 512
CONTEXT = 16384
N_CTX = 16
N_HEAD = 32


def draw_queries(key, part):
    key = jax.random.fold_in(key, 11)
    values = jax.random.normal(key, (TURN, Q_HEADS * HEAD_DIM), jnp.float32)
    return jnp.clip(values, -5.0, 5.0).astype(jnp.bfloat16)


def draw_cache_keys(key, part):
    key = jax.random.fold_in(key, 23)
    total_slots = SLOTS * N_CTX
    values = jax.random.normal(key, (N_HEAD, total_slots, HEAD_DIM), jnp.float32)
    return jnp.clip(values, -5.0, 5.0).astype(jnp.bfloat16)


def level_of(key, extent, cuts, smallest, largest):
    level, own = 1.0, jax.random.fold_in(key, 6)
    for axis_at, blocks in cuts:
        draws = jnp.exp(jax.random.uniform(jax.random.fold_in(own, axis_at), (blocks,), jnp.float32, smallest / len(cuts), largest / len(cuts)))
        level = level * jnp.repeat(draws, extent[axis_at] // blocks).reshape([-1 if axis == axis_at else 1 for axis in range(len(extent))])
    return level


def split_up(number_of, total, bound, slope):
    weights = [(1 << 20) // math.isqrt(grade ** slope) + 1 for grade in range(2, number_of + 1)]
    spare, counts = total - bound - (number_of - 1), [1] * (number_of - 1)
    while spare > 0:
        candidates = [i for i in range(number_of - 1) if counts[i] < bound]
        whole, remaining = sum([weights[i] for i in candidates]), spare
        for i in candidates:
            extra = min(bound - counts[i], max(1, remaining * weights[i] // whole), spare)
            counts[i] = counts[i] + extra
            spare = spare - extra
    return np.array([bound] + counts)


def ragged(stream_key, amount, total, bound, lean):
    if amount == 2:
        one = jax.random.randint(stream_key, (), max(1, total - bound), min(bound, total - 1) + 1)
        return jnp.stack([one, total - one])
    lengths = jnp.asarray(split_up(amount, total, bound, lean), jnp.int32)
    pairs = (amount - 1) // 2
    donor, taker = lengths[1:1 + 2 * pairs:2], lengths[2:2 + 2 * pairs:2]
    slack = jnp.minimum(donor - 1, bound - taker)
    passed = jax.random.randint(jax.random.fold_in(stream_key, 1), (pairs,), 0, 1 << 20) % (slack + 1)
    lengths = lengths.at[1:1 + 2 * pairs:2].set(donor - passed).at[2:2 + 2 * pairs:2].set(taker + passed)
    return lengths[jax.random.permutation(jax.random.fold_in(stream_key, 2), amount)]


def scatter_about(stream_key, shape, width, most, cuts=(), kind=jnp.bfloat16):
    values = width * jax.random.normal(stream_key, shape, jnp.float32)
    if cuts:
        values = values * level_of(stream_key, shape, cuts, -0.22, 0.18)
    return jnp.clip(values, -most, most).astype(kind)


def setup_inputs(seed: int = 0) -> dict:
    arg_keys = jax.random.split(jax.random.key(seed), 8)
    return {
        "queries": draw_queries(jax.random.fold_in(arg_keys[7], 71), 0),
        "cache_keys": draw_cache_keys(jax.random.fold_in(arg_keys[7], 71), 0),
        "cache_values": scatter_about(arg_keys[2], (N_HEAD, CONTEXT, HEAD_DIM), 1.0, 6.0, ((0, 32), (1, 16))),
        "turn_keys": scatter_about(arg_keys[3], (N_HEAD, TURN // KV_SHARERS, HEAD_DIM), 2.5, 12.0, ((0, 32), (1, 16))),
        "turn_values": scatter_about(arg_keys[4], (N_HEAD, TURN // KV_SHARERS, HEAD_DIM), 1.0, 6.0, ((0, 32), (1, 16))),
        "cache_fill": ragged(arg_keys[5], N_CTX, SLOTS * N_CTX // 2, SLOTS, 1).astype(jnp.int32),
        "turn_positions": jax.random.permutation(arg_keys[6], TURN).astype(jnp.int32),
    }


NEGATIVE = -1e+30

def attend(block_q, keys, values, visible, scale):
    scores = jnp.einsum('tgd,kd->tgk', block_q.astype(jnp.float32), keys.astype(jnp.float32)) * scale
    masked = jnp.where(visible[:, None, :], scores, NEGATIVE)
    peak = lax.optimization_barrier(jnp.max(masked, axis=2))
    weights = jnp.where(visible[:, None, :], jnp.exp(masked - peak[:, :, None]), 0.0)
    total = lax.optimization_barrier(jnp.sum(weights, axis=2))
    rounded = lax.optimization_barrier(weights.astype(jnp.bfloat16)).astype(jnp.float32)
    mixed = jnp.einsum('tgk,kd->tgd', rounded, values.astype(jnp.float32))
    return (mixed, peak, total)

def combine(first, second):
    peak = jnp.maximum(first[1], second[1])
    left = jnp.exp(first[1] - peak)
    right = jnp.exp(second[1] - peak)
    mixed = first[0] * left[:, :, None] + second[0] * right[:, :, None]
    return (mixed, peak, first[2] * left + second[2] * right)

def reference(queries, cache_keys, cache_values, turn_keys, turn_values, cache_fill, turn_positions):
    group = Q_HEADS // KV_HEADS
    parts = N_HEAD // KV_HEADS
    scale = 1.0 / math.sqrt(HEAD_DIM)
    slot_index = jnp.arange(SLOTS, dtype=jnp.int32)
    fills = jnp.tile(cache_fill, parts)
    causal = turn_positions[None, :] <= turn_positions[:, None]

    def one_head(index):
        start = (index * group * HEAD_DIM).astype(jnp.int32)
        block_q = lax.dynamic_slice_in_dim(queries, start, group * HEAD_DIM, 1).reshape(TURN, group, HEAD_DIM)
        first_row = (index * parts).astype(jnp.int32)
        keys = lax.dynamic_slice_in_dim(cache_keys, first_row, parts, 0).reshape(parts * N_CTX, SLOTS, HEAD_DIM)
        values = lax.dynamic_slice_in_dim(cache_values, first_row, parts, 0).reshape(parts * N_CTX, SLOTS, HEAD_DIM)
        fresh_k = lax.dynamic_slice_in_dim(turn_keys, first_row, parts, 0).reshape(TURN, HEAD_DIM)
        fresh_v = lax.dynamic_slice_in_dim(turn_values, first_row, parts, 0).reshape(TURN, HEAD_DIM)

        def step(carry, block):
            block_k, block_v, fill = block
            visible = jnp.broadcast_to((slot_index < fill)[None, :], (TURN, SLOTS))
            return (combine(carry, attend(block_q, block_k, block_v, visible, scale)), None)
        init = (jnp.zeros((TURN, group, HEAD_DIM), jnp.float32), jnp.full((TURN, group), NEGATIVE, jnp.float32), jnp.zeros((TURN, group), jnp.float32))
        carry, _ = lax.scan(step, init, (keys, values, fills))
        mixed, peak, total = combine(carry, attend(block_q, fresh_k, fresh_v, causal, scale))
        return (mixed / total[:, :, None]).reshape(TURN, group * HEAD_DIM)
    heads = lax.map(one_head, jnp.arange(KV_HEADS, dtype=jnp.int32))
    return jnp.transpose(heads, (1, 0, 2)).reshape(TURN, Q_HEADS * HEAD_DIM).astype(jnp.bfloat16)
```

```python
import functools
import math

import jax
import jax.numpy as jnp
from jax import lax
from jax.experimental import pallas as pl
from jax.experimental.pallas import tpu as pltpu
from jax.sharding import PartitionSpec as P

Q_HEADS = 96
KV_HEADS = 8
NEGATIVE = -1e30
STEP = 256
TILE = 4
STAT_ROWS = 16

VMEM = pl.BlockSpec(memory_space=pltpu.VMEM)
SMEM = pl.BlockSpec(memory_space=pltpu.SMEM)


def prepare_kernel(fill_ref, k_ref, v_ref, tk_ref, tv_ref, kv_ref):
    slots, width = k_ref.shape
    turn = tk_ref.shape[0]
    fill = fill_ref[0]
    ok = lax.broadcasted_iota(jnp.int32, (slots, width), 0) < fill
    first = jnp.broadcast_to(k_ref[0:1, :].astype(jnp.float32), (slots, width))
    kv_ref[0:slots, :] = jnp.where(ok, k_ref[...].astype(jnp.float32), first).astype(jnp.bfloat16)
    kv_ref[slots : 2 * slots, :] = jnp.where(ok, v_ref[...].astype(jnp.float32), 0.0).astype(jnp.bfloat16)
    kv_ref[2 * slots : 2 * slots + 2 * turn, :] = jnp.concatenate([tk_ref[...], tv_ref[...]], axis=0)


def bias_kernel(index_ref, pos_smem, pos_ref, bias_ref):
    blocks, width = pos_ref.shape
    ctx, sub = index_ref[0], index_ref[1]
    lane = lax.broadcasted_iota(jnp.int32, (1, width), 1)
    keys = jnp.full((1, width), 1 << 20, jnp.int32)
    for n, flip in enumerate((0, 2, 1, 3)):
        base = (sub ^ flip) * width + ctx * 8
        for i in range(8):
            keys = jnp.where(lane == n * 8 + i, pos_smem[base + i], keys)
    keys = keys.astype(jnp.float32)
    pos = pos_ref[...].astype(jnp.float32)
    for b in range(blocks):
        tokens = jnp.broadcast_to(pos[b : b + 1, :], (width, width)).T
        bias_ref[b * width : (b + 1) * width, :] = jnp.where(keys <= tokens, 0.0, NEGATIVE)


def attend_kernel(fill_ref, q_ref, a_ref, b_ref, c_ref, d_ref, bias_ref, out_ref, *, slots, turn):
    sources = (a_ref, b_ref, c_ref, d_ref)
    blocks, tokens, columns = q_ref.shape
    width = a_ref.shape[1]
    heads = columns // width
    rows = heads * tokens
    factor = math.log2(math.e) / math.sqrt(width)
    fill = fill_ref[0]
    steps = (fill + (STEP - 1)) // STEP
    contract = (((1,), (1,)), ((), ()))
    plain = (((1,), (0,)), ((), ()))

    def scored(q, keys):
        return lax.dot_general(q, keys, contract, preferred_element_type=jnp.float32)

    def flags(start):
        at = lax.broadcasted_iota(jnp.int32, (STEP, width), 0) + start
        return jnp.where(at < fill, 1.0, 0.0).astype(jnp.bfloat16)

    def weighted(scores, peak, values):
        weights = jnp.exp2(scores - peak).astype(jnp.bfloat16)
        return lax.dot_general(weights, values, plain, preferred_element_type=jnp.float32)

    turn_k = jnp.concatenate([s[2 * slots : 2 * slots + 2 * turn, :][:turn] for s in sources], axis=0)
    turn_v = jnp.concatenate([s[2 * slots : 2 * slots + 2 * turn, :][turn:] for s in sources], axis=0)
    count = turn * len(sources)
    turn_va = jnp.concatenate([turn_v, jnp.ones((count, width), jnp.bfloat16)], axis=1)

    def tile(at, _):
        q = jnp.concatenate(
            [q_ref[at * TILE + n, :, h * width : (h + 1) * width] for n in range(TILE) for h in range(heads)], axis=0
        )
        bias = jnp.concatenate(
            [
                bias_ref[pl.ds(pl.multiple_of((at * TILE + n) * tokens, tokens), tokens), 0:count]
                for n in range(TILE)
                for h in range(heads)
            ],
            axis=0,
        )

        def step(start):
            return [scored(q, s[pl.ds(start, STEP), :]) * factor for s in sources]

        def peak_of(scores):
            best = functools.reduce(jnp.maximum, scores)
            return jnp.max(best, axis=1, keepdims=True)

        def mixed(scores, peak, start):
            flag = flags(start)
            return sum(
                weighted(
                    x,
                    peak,
                    jnp.concatenate([s[pl.ds(pl.multiple_of(slots + start, STEP), STEP), :], flag], axis=1),
                )
                for x, s in zip(scores, sources)
            )

        scores = step(0)
        fresh = scored(q, turn_k) * factor + bias
        peak = jnp.maximum(peak_of(scores), jnp.max(fresh, axis=1, keepdims=True))
        total = mixed(scores, peak, 0) + weighted(fresh, peak, turn_va)

        def more(j, state):
            total, peak = state
            start = pl.multiple_of(j * STEP, STEP)
            scores = step(start)
            best = jnp.maximum(peak, peak_of(scores))
            return total * jnp.exp2(peak - best) + mixed(scores, best, start), best

        total, peak = lax.fori_loop(1, steps, more, (total, peak))
        norm = total[:, width:]
        result = (total[:, :width] / norm).astype(jnp.bfloat16)
        lse = peak + jnp.log2(norm)
        row = lax.broadcasted_iota(jnp.int32, (rows, width), 0)
        lane = lax.broadcasted_iota(jnp.int32, (rows, width), 1)
        stat_row = lax.broadcasted_iota(jnp.int32, (STAT_ROWS, width), 0)
        for n in range(TILE):
            out_ref[at * TILE + n, 0:rows, :] = result[n * rows : (n + 1) * rows]
            flat = jnp.sum(jnp.where(row == lane, lse[n * rows : (n + 1) * rows], 0.0), axis=0, keepdims=True)
            high = flat.astype(jnp.bfloat16).astype(jnp.float32)
            middle = (flat - high).astype(jnp.bfloat16).astype(jnp.float32)
            low = flat - high - middle
            stat = jnp.where(
                stat_row == 0, high, jnp.where(stat_row == 1, middle, jnp.where(stat_row == 2, low, 0.0))
            )
            out_ref[at * TILE + n, rows : rows + STAT_ROWS, :] = stat.astype(jnp.bfloat16)
        return 0

    lax.fori_loop(0, blocks // TILE, tile, 0)


def combine_kernel(part_ref, out_ref):
    blocks, _, width = part_ref.shape
    tokens, columns = out_ref.shape
    heads = columns // width
    rows = heads * tokens
    pieces = [part_ref[c, rows : rows + STAT_ROWS, :].astype(jnp.float32) for c in range(blocks)]
    lse = jnp.concatenate([p[0:1] + p[1:2] + p[2:3] for p in pieces], axis=0)
    share = jnp.exp2(lse - jnp.max(lse, axis=0, keepdims=True))
    share = share / jnp.sum(share, axis=0, keepdims=True)
    share = jnp.concatenate([share, jnp.zeros((width - blocks, width), jnp.float32)], axis=0).T
    total = jnp.zeros((rows, width), jnp.float32)
    for c in range(blocks):
        total = total + part_ref[c, 0:rows, :].astype(jnp.float32) * share[0:rows, c : c + 1]
    total = total.astype(jnp.bfloat16)
    for h in range(heads):
        out_ref[:, h * width : (h + 1) * width] = total[h * tokens : (h + 1) * tokens]


def prepare(fill, keys, values, turn_k, turn_v):
    slots, width = keys.shape
    return pl.pallas_call(
        prepare_kernel,
        out_shape=jax.ShapeDtypeStruct((2 * slots + 2 * turn_k.shape[0], width), jnp.bfloat16),
        in_specs=[SMEM] + [VMEM] * 4,
        out_specs=VMEM,
        name="prepare",
    )(fill, keys, values, turn_k, turn_v)


def bias_of(index, positions, width):
    return pl.pallas_call(
        bias_kernel,
        out_shape=jax.ShapeDtypeStruct((positions.shape[0], width), jnp.float32),
        in_specs=[SMEM, SMEM, VMEM],
        out_specs=VMEM,
        name="bias",
    )(index, positions, positions.reshape(-1, width))


def attend(fill, q, sources, bias, slots, turn):
    blocks, tokens, columns = q.shape
    width = bias.shape[1]
    rows = tokens * columns // width
    work = blocks * rows * slots * len(sources)
    return pl.pallas_call(
        functools.partial(attend_kernel, slots=slots, turn=turn),
        out_shape=jax.ShapeDtypeStruct((blocks, rows + STAT_ROWS, width), jnp.bfloat16),
        in_specs=[SMEM] + [VMEM] * 6,
        out_specs=VMEM,
        compiler_params=pltpu.CompilerParams(vmem_limit_bytes=48 * 1024 * 1024),
        cost_estimate=pl.CostEstimate(flops=4 * work * width, bytes_accessed=4 << 20, transcendentals=work),
        name="attend",
    )(fill, q, *sources, bias)


def combine(parts, tokens, columns):
    return pl.pallas_call(
        combine_kernel,
        out_shape=jax.ShapeDtypeStruct((tokens, columns), jnp.bfloat16),
        in_specs=[VMEM],
        out_specs=VMEM,
        name="combine",
    )(parts)


def body(queries, cache_keys, cache_values, turn_keys, turn_values, cache_fill, turn_positions):
    tokens, columns = queries.shape
    width = cache_keys.shape[2]
    slots = cache_keys.shape[1]
    turn = turn_keys.shape[1]
    n_ctx, n_head = lax.axis_size("ctx"), lax.axis_size("head")
    sub = lax.axis_index("head") % (n_head // KV_HEADS)
    index = jnp.stack([lax.axis_index("ctx"), sub]).astype(jnp.int32)
    other = [(i, i ^ 1) for i in range(n_head)]
    across = [(i, i ^ 2) for i in range(n_head)]

    copies = jnp.broadcast_to(queries[None], (n_ctx, tokens, columns))
    q = lax.all_to_all(copies, "ctx", split_axis=0, concat_axis=0, tiled=True)
    own = prepare(cache_fill, cache_keys[0], cache_values[0], turn_keys[0], turn_values[0])
    far = lax.ppermute(own, "head", across)
    near = lax.ppermute(own, "head", other)
    diagonal = lax.ppermute(far, "head", other)
    bias = bias_of(index, turn_positions, width)
    parts = attend(cache_fill, q, (own, far, near, diagonal), bias, slots, turn)
    parts = lax.all_to_all(parts, "ctx", split_axis=0, concat_axis=0, tiled=True)
    return combine(parts, tokens, columns)


def solution(mesh):
    in_specs = (
        P("ctx", "head"),
        P("head", "ctx", None),
        P("head", "ctx", None),
        P("head", "ctx", None),
        P("head", "ctx", None),
        P("ctx"),
        P(),
    )
    return jax.shard_map(body, mesh=mesh, in_specs=in_specs, out_specs=P("ctx", "head"), check_vma=False)
```

```python
import functools
import math

import jax
import jax.numpy as jnp
from jax import lax
from jax.experimental import pallas as pl
from jax.experimental.pallas import tpu as pltpu
from jax.sharding import PartitionSpec as P

Q_HEADS = 96
KV_HEADS = 8
NEGATIVE = -1e30
STEP = 512
TILE = 2
AHEAD = 3
KERNEL_VMEM = 24 * 1024 * 1024
STAT_ROWS = 16

VMEM = pl.BlockSpec(memory_space=pltpu.VMEM)
SMEM = pl.BlockSpec(memory_space=pltpu.SMEM)


def prepare_kernel(fill_ref, k_ref, v_ref, tk_ref, tv_ref, kv_ref):
    slots, width = k_ref.shape
    turn = tk_ref.shape[0]
    fill = fill_ref[0]
    first = jnp.broadcast_to(k_ref[0:1, :].astype(jnp.float32), (width, width))
    for at in range(0, slots, width):
        ok = lax.broadcasted_iota(jnp.int32, (width, width), 0) + at < fill
        keys = jnp.where(ok, k_ref[at : at + width, :].astype(jnp.float32), first)
        kv_ref[at : at + width, :] = keys.T.astype(jnp.bfloat16)
        values = jnp.where(ok, v_ref[at : at + width, :].astype(jnp.float32), 0.0)
        kv_ref[slots + at : slots + at + width, :] = values.astype(jnp.bfloat16)
    kv_ref[2 * slots : 2 * slots + 2 * turn, :] = jnp.concatenate([tk_ref[...], tv_ref[...]], axis=0)


def bias_kernel(index_ref, pos_smem, pos_ref, bias_ref):
    blocks, width = pos_ref.shape
    ctx, sub = index_ref[0], index_ref[1]
    lane = lax.broadcasted_iota(jnp.int32, (1, width), 1)
    keys = jnp.full((1, width), 1 << 20, jnp.int32)
    for n, flip in enumerate((0, 2, 1, 3)):
        base = (sub ^ flip) * width + ctx * 8
        for i in range(8):
            keys = jnp.where(lane == n * 8 + i, pos_smem[base + i], keys)
    keys = keys.astype(jnp.float32)
    pos = pos_ref[...].astype(jnp.float32)
    for b in range(blocks):
        tokens = jnp.broadcast_to(pos[b : b + 1, :], (width, width)).T
        bias_ref[b * width : (b + 1) * width, :] = jnp.where(keys <= tokens, 0.0, NEGATIVE)


def attend_kernel(
    fill_ref, q_ref, a_ref, b_ref, c_ref, d_ref, bias_ref, out_ref, total_ref, peak_ref, *, slots, turn
):
    sources = (a_ref, b_ref, c_ref, d_ref)
    blocks, tokens, columns = q_ref.shape
    width = a_ref.shape[1]
    heads = columns // width
    rows = heads * tokens
    size = TILE * rows
    tiles = blocks // TILE
    count = turn * len(sources)
    factor = math.log2(math.e) / math.sqrt(width)
    fill = fill_ref[0]
    plain = (((1,), (0,)), ((), ()))
    contract = (((1,), (1,)), ((), ()))

    def dot(first, second, dims=plain):
        return lax.dot_general(first, second, dims, preferred_element_type=jnp.float32)

    def weights(scores, peak):
        return jnp.exp2(scores * factor - peak).astype(jnp.bfloat16)

    def turned(index):
        pairs = [s[2 * slots : 2 * slots + 2 * turn, :] for s in sources]
        return jnp.concatenate([p[index * turn : (index + 1) * turn] for p in pairs], axis=0)

    turn_k = turned(0)
    turn_v = jnp.concatenate([turned(1), jnp.ones((count, width), jnp.bfloat16)], axis=1)

    row = lax.broadcasted_iota(jnp.int32, (rows, width), 0)
    lane = lax.broadcasted_iota(jnp.int32, (rows, width), 1)
    stat_row = lax.broadcasted_iota(jnp.int32, (STAT_ROWS, width), 0)

    def finish(t, total, peak):
        for n in range(TILE):
            at = t * TILE + n
            part = total[n * rows : (n + 1) * rows]
            norm = part[:, width:]
            out_ref[at, 0:rows, :] = (part[:, :width] / norm).astype(jnp.bfloat16)
            lse = peak[n * rows : (n + 1) * rows] + jnp.log2(norm)
            flat = jnp.sum(jnp.where(row == lane, lse, 0.0), axis=0, keepdims=True)
            high = flat.astype(jnp.bfloat16).astype(jnp.float32)
            middle = (flat - high).astype(jnp.bfloat16).astype(jnp.float32)
            low = flat - high - middle
            stat = jnp.where(
                stat_row == 0, high, jnp.where(stat_row == 1, middle, jnp.where(stat_row == 2, low, 0.0))
            )
            out_ref[at, rows : rows + STAT_ROWS, :] = stat.astype(jnp.bfloat16)

    def step(start, first, last):
        keys = jnp.concatenate([s[start + b : start + b + width, :] for s in sources for b in range(0, STEP, width)], axis=1)
        slot = lax.broadcasted_iota(jnp.int32, (STEP, width), 0) + start
        flag = jnp.where(slot < fill, 1.0, 0.0).astype(jnp.bfloat16)
        values = jnp.concatenate(
            [jnp.concatenate([s[slots + start : slots + start + STEP, :], flag], axis=1) for s in sources], axis=0
        )

        def score(t):
            q = jnp.concatenate(
                [q_ref[t * TILE + n, :, h * width : (h + 1) * width] for n in range(TILE) for h in range(heads)],
                axis=0,
            )
            if not first:
                return dot(q, keys), None
            bias = jnp.concatenate(
                [
                    bias_ref[(t * TILE + n) * tokens : (t * TILE + n + 1) * tokens, 0:count]
                    for n in range(TILE)
                    for h in range(heads)
                ],
                axis=0,
            )
            return dot(q, keys), dot(q, turn_k, contract) + bias

        def mix(t, scores, fresh):
            at = slice(t * size, (t + 1) * size)
            peak = jnp.max(scores, axis=1, keepdims=True)
            if first:
                peak = jnp.maximum(peak, jnp.max(fresh, axis=1, keepdims=True)) * factor
                total = dot(weights(scores, peak), values) + dot(weights(fresh, peak), turn_v)
            else:
                before = peak_ref[at, 0:1]
                peak = jnp.maximum(before, peak * factor)
                total = total_ref[at, :] * jnp.exp2(before - peak) + dot(weights(scores, peak), values)
            if last:
                finish(t, total, peak)
            else:
                total_ref[at, :] = total
                peak_ref[at, :] = jnp.broadcast_to(peak, (size, width))

        ahead = []
        for t in range(tiles):
            ahead.append((t, *score(t)))
            if len(ahead) > AHEAD:
                mix(*ahead.pop(0))
        for waiting in ahead:
            mix(*waiting)

    @pl.when(fill <= STEP)
    def _():
        step(0, True, True)

    @pl.when(fill > STEP)
    def _():
        for start in range(0, slots, STEP):
            step(start, start == 0, start + STEP == slots)


def combine_kernel(part_ref, out_ref):
    blocks, _, width = part_ref.shape
    tokens, columns = out_ref.shape
    heads = columns // width
    rows = heads * tokens
    pieces = [part_ref[c, rows : rows + STAT_ROWS, :].astype(jnp.float32) for c in range(blocks)]
    lse = jnp.concatenate([p[0:1] + p[1:2] + p[2:3] for p in pieces], axis=0)
    share = jnp.exp2(lse - jnp.max(lse, axis=0, keepdims=True))
    share = share / jnp.sum(share, axis=0, keepdims=True)
    share = jnp.concatenate([share, jnp.zeros((width - blocks, width), jnp.float32)], axis=0).T
    total = jnp.zeros((rows, width), jnp.float32)
    for c in range(blocks):
        total = total + part_ref[c, 0:rows, :].astype(jnp.float32) * share[0:rows, c : c + 1]
    total = total.astype(jnp.bfloat16)
    for h in range(heads):
        out_ref[:, h * width : (h + 1) * width] = total[h * tokens : (h + 1) * tokens]


def prepare(fill, keys, values, turn_k, turn_v):
    slots, width = keys.shape
    return pl.pallas_call(
        prepare_kernel,
        out_shape=jax.ShapeDtypeStruct((2 * slots + 2 * turn_k.shape[0], width), jnp.bfloat16),
        in_specs=[SMEM] + [VMEM] * 4,
        out_specs=VMEM,
        name="prepare",
    )(fill, keys, values, turn_k, turn_v)


def bias_of(index, positions, width):
    return pl.pallas_call(
        bias_kernel,
        out_shape=jax.ShapeDtypeStruct((positions.shape[0], width), jnp.float32),
        in_specs=[SMEM, SMEM, VMEM],
        out_specs=VMEM,
        name="bias",
    )(index, positions, positions.reshape(-1, width))


def attend(fill, q, sources, bias, slots, turn):
    blocks, tokens, columns = q.shape
    width = bias.shape[1]
    rows = tokens * columns // width
    work = blocks * rows * slots * len(sources)
    return pl.pallas_call(
        functools.partial(attend_kernel, slots=slots, turn=turn),
        out_shape=jax.ShapeDtypeStruct((blocks, rows + STAT_ROWS, width), jnp.bfloat16),
        in_specs=[SMEM] + [VMEM] * 6,
        out_specs=VMEM,
        scratch_shapes=[
            pltpu.VMEM((blocks * rows, 2 * width), jnp.float32),
            pltpu.VMEM((blocks * rows, width), jnp.float32),
        ],
        compiler_params=pltpu.CompilerParams(vmem_limit_bytes=KERNEL_VMEM),
        cost_estimate=pl.CostEstimate(flops=4 * work * width, bytes_accessed=4 << 20, transcendentals=work),
        name="attend",
    )(fill, q, *sources, bias)


def combine(parts, tokens, columns):
    return pl.pallas_call(
        combine_kernel,
        out_shape=jax.ShapeDtypeStruct((tokens, columns), jnp.bfloat16),
        in_specs=[VMEM],
        out_specs=VMEM,
        name="combine",
    )(parts)


def body(queries, cache_keys, cache_values, turn_keys, turn_values, cache_fill, turn_positions):
    tokens, columns = queries.shape
    width = cache_keys.shape[2]
    slots = cache_keys.shape[1]
    turn = turn_keys.shape[1]
    n_ctx, n_head = lax.axis_size("ctx"), lax.axis_size("head")
    sub = lax.axis_index("head") % (n_head // KV_HEADS)
    index = jnp.stack([lax.axis_index("ctx"), sub]).astype(jnp.int32)
    other = [(i, i ^ 1) for i in range(n_head)]
    across = [(i, i ^ 2) for i in range(n_head)]

    copies = jnp.broadcast_to(queries[None], (n_ctx, tokens, columns))
    copies, cache_fill = lax.optimization_barrier((copies, cache_fill))
    q = lax.all_to_all(copies, "ctx", split_axis=0, concat_axis=0, tiled=True)
    own = prepare(cache_fill, cache_keys[0], cache_values[0], turn_keys[0], turn_values[0])
    far = lax.ppermute(own, "head", across)
    near = lax.ppermute(own, "head", other)
    diagonal = lax.ppermute(far, "head", other)
    bias = bias_of(index, turn_positions, width)
    parts = attend(cache_fill, q, (own, far, near, diagonal), bias, slots, turn)
    parts = lax.all_to_all(parts, "ctx", split_axis=0, concat_axis=0, tiled=True)
    return combine(parts, tokens, columns)


def solution(mesh):
    in_specs = (
        P("ctx", "head"),
        P("head", "ctx", None),
        P("head", "ctx", None),
        P("head", "ctx", None),
        P("head", "ctx", None),
        P("ctx"),
        P(),
    )
    return jax.shard_map(body, mesh=mesh, in_specs=in_specs, out_specs=P("ctx", "head"), check_vma=False)
```

```python
import functools
import math

import jax
import jax.numpy as jnp
from jax import lax
from jax.experimental import pallas as pl
from jax.experimental.pallas import tpu as pltpu
from jax.sharding import PartitionSpec as P

Q_HEADS = 96
KV_HEADS = 8
NEGATIVE = -1e30
STEP = 512
TILE = 2
AHEAD = 3
KERNEL_VMEM = 24 * 1024 * 1024
STAT_ROWS = 16
META_ROWS = 16

VMEM = pl.BlockSpec(memory_space=pltpu.VMEM)
SMEM = pl.BlockSpec(memory_space=pltpu.SMEM)
HBM = pl.BlockSpec(memory_space=pltpu.HBM)


def prepare_kernel(
    fill_ref, q_hbm, k_hbm, v_hbm, tk_hbm, tv_hbm, spread_ref, kv_ref, q_ref, k_ref, v_ref, turn_ref, sems
):
    slots, width = k_ref.shape
    turn = tk_hbm.shape[0]
    pairs = (
        (k_hbm, k_ref),
        (v_hbm, v_ref),
        (q_hbm, q_ref),
        (tk_hbm, turn_ref.at[0]),
        (tv_hbm, turn_ref.at[1]),
    )
    moves = [pltpu.make_async_copy(src, dst, sems.at[n]) for n, (src, dst) in enumerate(pairs)]
    for move in moves:
        move.start()
    fill = jnp.broadcast_to(fill_ref[...], (width, width))
    moves[0].wait()
    first = jnp.broadcast_to(k_ref[0:1, :].astype(jnp.float32), (width, width))
    row = lax.broadcasted_iota(jnp.int32, (width, width), 0)
    for at in range(0, slots, width):
        keys = jnp.where(row + at < fill, k_ref[at : at + width, :].astype(jnp.float32), first)
        kv_ref[at : at + width, :] = keys.T.astype(jnp.bfloat16)
    moves[1].wait()
    for at in range(0, slots, width):
        values = jnp.where(row + at < fill, v_ref[at : at + width, :].astype(jnp.float32), 0.0)
        kv_ref[slots + at : slots + at + width, :] = values.astype(jnp.bfloat16)
    moves[2].wait()
    for at in range(spread_ref.shape[0]):
        spread_ref[at] = q_ref[...]
    moves[3].wait()
    moves[4].wait()
    at = 2 * slots
    kv_ref[at : at + 2 * turn, :] = jnp.concatenate([turn_ref[0], turn_ref[1]], axis=0)
    at += 2 * turn
    half = lax.broadcasted_iota(jnp.int32, (META_ROWS, width), 0) < META_ROWS // 2
    meta = jnp.where(half, fill[:META_ROWS] >> 5, fill[:META_ROWS] & 31)
    kv_ref[at : at + META_ROWS, :] = meta.astype(jnp.float32).astype(jnp.bfloat16)


def bias_kernel(index_ref, pos_smem, pos_ref, bias_ref):
    blocks, width = pos_ref.shape
    ctx, sub = index_ref[0], index_ref[1]
    lane = lax.broadcasted_iota(jnp.int32, (1, width), 1)
    keys = jnp.full((1, width), 1 << 20, jnp.int32)
    core = sub % 2
    for n, (at, flip) in enumerate(((ctx, 0), (ctx, 1), (ctx ^ core, 2), (ctx ^ 1 ^ core, 3))):
        for i in range(8):
            keys = jnp.where(lane == n * 8 + i, pos_smem[(sub ^ flip) * width + at * 8 + i], keys)
    keys = keys.astype(jnp.float32)
    pos = pos_ref[...].astype(jnp.float32)
    for b in range(blocks):
        tokens = jnp.broadcast_to(pos[b : b + 1, :], (width, width)).T
        bias_ref[b * width : (b + 1) * width, :] = jnp.where(keys <= tokens, 0.0, NEGATIVE)


def attend_kernel(
    q_ref, own_ref, near_ref, far_ref, diagonal_ref, bias_ref, out_ref, total_ref, peak_ref, *, slots, turn
):
    sources = (own_ref, near_ref, far_ref, diagonal_ref)
    blocks, tokens, columns = q_ref.shape
    width = own_ref.shape[1]
    heads = columns // width
    rows = heads * tokens
    size = TILE * rows
    tiles = blocks // TILE
    count = turn * len(sources)
    factor = math.log2(math.e) / math.sqrt(width)
    plain = (((1,), (0,)), ((), ()))
    contract = (((1,), (1,)), ((), ()))

    def dot(first, second, dims=plain):
        return lax.dot_general(first, second, dims, preferred_element_type=jnp.float32)

    def weights(scores, peak):
        return jnp.exp2(scores * factor - peak).astype(jnp.bfloat16)

    def visible(source, start):
        meta = source[2 * slots + 2 * turn :, :].astype(jnp.float32)
        half = META_ROWS // 2
        fill = meta[0:1] * 32 + meta[half : half + 1]
        slot = lax.broadcasted_iota(jnp.int32, (STEP, width), 0) + start
        return jnp.where(slot.astype(jnp.float32) < fill, 1.0, 0.0).astype(jnp.bfloat16)

    def turned(index):
        pairs = [s[2 * slots : 2 * slots + 2 * turn, :] for s in sources]
        return jnp.concatenate([p[index * turn : (index + 1) * turn] for p in pairs], axis=0)

    turn_k = turned(0)
    turn_v = jnp.concatenate([turned(1), jnp.ones((count, width), jnp.bfloat16)], axis=1)

    row = lax.broadcasted_iota(jnp.int32, (rows, width), 0)
    lane = lax.broadcasted_iota(jnp.int32, (rows, width), 1)
    stat_row = lax.broadcasted_iota(jnp.int32, (STAT_ROWS, width), 0)

    def finish(t, total, peak):
        for n in range(TILE):
            at = t * TILE + n
            part = total[n * rows : (n + 1) * rows]
            norm = part[:, width:]
            out_ref[at, 0:rows, :] = (part[:, :width] / norm).astype(jnp.bfloat16)
            lse = peak[n * rows : (n + 1) * rows] + jnp.log2(norm)
            flat = jnp.sum(jnp.where(row == lane, lse, 0.0), axis=0, keepdims=True)
            high = flat.astype(jnp.bfloat16).astype(jnp.float32)
            middle = (flat - high).astype(jnp.bfloat16).astype(jnp.float32)
            low = flat - high - middle
            stat = jnp.where(
                stat_row == 0, high, jnp.where(stat_row == 1, middle, jnp.where(stat_row == 2, low, 0.0))
            )
            out_ref[at, rows : rows + STAT_ROWS, :] = stat.astype(jnp.bfloat16)

    def step(start, taken, first, last):
        keys = jnp.concatenate(
            [s[start + b : start + b + width, :] for s in taken for b in range(0, STEP, width)], axis=1
        )
        values = jnp.concatenate(
            [
                jnp.concatenate([s[slots + start : slots + start + STEP, :], visible(s, start)], axis=1)
                for s in taken
            ],
            axis=0,
        )

        def score(t):
            q = jnp.concatenate(
                [q_ref[t * TILE + n, :, h * width : (h + 1) * width] for n in range(TILE) for h in range(heads)],
                axis=0,
            )
            if not first:
                return dot(q, keys), None
            bias = jnp.concatenate(
                [
                    bias_ref[(t * TILE + n) * tokens : (t * TILE + n + 1) * tokens, 0:count]
                    for n in range(TILE)
                    for h in range(heads)
                ],
                axis=0,
            )
            return dot(q, keys), dot(q, turn_k, contract) + bias

        def mix(t, scores, fresh):
            at = slice(t * size, (t + 1) * size)
            peak = jnp.max(scores, axis=1, keepdims=True)
            if first:
                peak = jnp.maximum(peak, jnp.max(fresh, axis=1, keepdims=True)) * factor
                total = dot(weights(scores, peak), values) + dot(weights(fresh, peak), turn_v)
            else:
                before = peak_ref[at, 0:1]
                peak = jnp.maximum(before, peak * factor)
                total = total_ref[at, :] * jnp.exp2(before - peak) + dot(weights(scores, peak), values)
            if last:
                finish(t, total, peak)
            else:
                total_ref[at, :] = total
                peak_ref[at, :] = jnp.broadcast_to(peak, (size, width))

        ahead = []
        for t in range(tiles):
            ahead.append((t, *score(t)))
            if len(ahead) > AHEAD:
                mix(*ahead.pop(0))
        for waiting in ahead:
            mix(*waiting)

    def more(source):
        meta = source[2 * slots + 2 * turn :, :].astype(jnp.float32)
        half = META_ROWS // 2
        return jnp.max(meta[:half]) * 32 + jnp.max(meta[half:]) > STEP

    wide = [more(s) for s in (own_ref, far_ref, diagonal_ref)]
    step(0, sources, True, False)

    for mine, first, second in ((0, 0, 0), (0, 0, 1), (0, 1, 0), (1, 0, 1), (1, 1, 0), (1, 1, 1)):
        rest = sources[:2] * mine + sources[2:3] * first + sources[3:] * second
        given = [w if want else jnp.logical_not(w) for w, want in zip(wide, (mine, first, second))]

        @pl.when(given[0] & given[1] & given[2])
        def _(rest=rest):
            if rest:
                step(STEP, rest, False, True)
            else:
                for t in range(tiles):
                    at = slice(t * size, (t + 1) * size)
                    finish(t, total_ref[at, :], peak_ref[at, :])


def combine_kernel(part_ref, out_ref):
    blocks, _, width = part_ref.shape
    tokens, columns = out_ref.shape
    heads = columns // width
    rows = heads * tokens
    pieces = [part_ref[c, rows : rows + STAT_ROWS, :].astype(jnp.float32) for c in range(blocks)]
    lse = jnp.concatenate([p[0:1] + p[1:2] + p[2:3] for p in pieces], axis=0)
    share = jnp.exp2(lse - jnp.max(lse, axis=0, keepdims=True))
    share = share / jnp.sum(share, axis=0, keepdims=True)
    share = jnp.concatenate([share, jnp.zeros((width - blocks, width), jnp.float32)], axis=0).T
    total = jnp.zeros((rows, width), jnp.float32)
    for c in range(blocks):
        total = total + part_ref[c, 0:rows, :].astype(jnp.float32) * share[0:rows, c : c + 1]
    total = total.astype(jnp.bfloat16)
    for h in range(heads):
        out_ref[:, h * width : (h + 1) * width] = total[h * tokens : (h + 1) * tokens]


def prepare(fill, queries, keys, values, turn_k, turn_v, copies):
    slots, width = keys.shape
    turn = turn_k.shape[0]
    return pl.pallas_call(
        prepare_kernel,
        out_shape=[
            jax.ShapeDtypeStruct((copies, *queries.shape), jnp.bfloat16),
            jax.ShapeDtypeStruct((2 * slots + 2 * turn + META_ROWS, width), jnp.bfloat16),
        ],
        in_specs=[VMEM] + [HBM] * 5,
        out_specs=[VMEM, VMEM],
        scratch_shapes=[
            pltpu.VMEM(queries.shape, jnp.bfloat16),
            pltpu.VMEM(keys.shape, jnp.bfloat16),
            pltpu.VMEM(values.shape, jnp.bfloat16),
            pltpu.VMEM((2, turn, width), jnp.bfloat16),
            pltpu.SemaphoreType.DMA((5,)),
        ],
        compiler_params=pltpu.CompilerParams(vmem_limit_bytes=56 * 1024 * 1024),
        name="prepare",
    )(fill.reshape(1, 1), queries, keys, values, turn_k, turn_v)


def bias_of(index, positions, width):
    return pl.pallas_call(
        bias_kernel,
        out_shape=jax.ShapeDtypeStruct((positions.shape[0], width), jnp.float32),
        in_specs=[SMEM, SMEM, VMEM],
        out_specs=VMEM,
        compiler_params=pltpu.CompilerParams(vmem_limit_bytes=4 * 1024 * 1024),
        name="bias",
    )(index, positions, positions.reshape(-1, width))


def attend(q, sources, bias, slots, turn):
    blocks, tokens, columns = q.shape
    width = sources[0].shape[1]
    rows = tokens * columns // width
    work = blocks * rows * slots * len(sources)
    return pl.pallas_call(
        functools.partial(attend_kernel, slots=slots, turn=turn),
        out_shape=jax.ShapeDtypeStruct((blocks, rows + STAT_ROWS, width), jnp.bfloat16),
        in_specs=[VMEM] * 6,
        out_specs=VMEM,
        scratch_shapes=[
            pltpu.VMEM((blocks * rows, 2 * width), jnp.float32),
            pltpu.VMEM((blocks * rows, width), jnp.float32),
        ],
        compiler_params=pltpu.CompilerParams(vmem_limit_bytes=KERNEL_VMEM),
        cost_estimate=pl.CostEstimate(flops=4 * work * width, bytes_accessed=4 << 20, transcendentals=work),
        name="attend",
    )(q, *sources, bias)


def combine(parts, tokens, columns):
    return pl.pallas_call(
        combine_kernel,
        out_shape=jax.ShapeDtypeStruct((tokens, columns), jnp.bfloat16),
        in_specs=[VMEM],
        out_specs=VMEM,
        compiler_params=pltpu.CompilerParams(vmem_limit_bytes=4 * 1024 * 1024),
        name="combine",
    )(parts)


def body(queries, cache_keys, cache_values, turn_keys, turn_values, cache_fill, turn_positions):
    tokens, columns = queries.shape
    width = cache_keys.shape[2]
    slots = cache_keys.shape[1]
    turn = turn_keys.shape[1]
    n_ctx, n_head = lax.axis_size("ctx"), lax.axis_size("head")
    sub = lax.axis_index("head") % (n_head // KV_HEADS)
    index = jnp.stack([lax.axis_index("ctx"), sub]).astype(jnp.int32)
    other = [(h, h ^ 1) for h in range(n_head)]
    across = [
        (c * n_head + h, (c ^ (h & 1)) * n_head + (h ^ 2)) for c in range(n_ctx) for h in range(n_head)
    ]

    copies, own = prepare(
        cache_fill, queries, cache_keys[0], cache_values[0], turn_keys[0], turn_values[0], n_ctx
    )
    q = lax.all_to_all(copies, "ctx", split_axis=0, concat_axis=0, tiled=True)
    far = lax.ppermute(own, ("ctx", "head"), across)
    near = lax.ppermute(own, "head", other)
    diagonal = lax.ppermute(far, "head", other)
    bias = bias_of(index, turn_positions, width)
    parts = attend(q, (own, near, far, diagonal), bias, slots, turn)
    parts = lax.all_to_all(parts, "ctx", split_axis=0, concat_axis=0, tiled=True)
    return combine(parts, tokens, columns)


def solution(mesh):
    in_specs = (
        P("ctx", "head"),
        P("head", "ctx", None),
        P("head", "ctx", None),
        P("head", "ctx", None),
        P("head", "ctx", None),
        P("ctx"),
        P(),
    )
    return jax.shard_map(body, mesh=mesh, in_specs=in_specs, out_specs=P("ctx", "head"), check_vma=False)
```

```python
import functools
import math

import jax
import jax.numpy as jnp
from jax import lax
from jax.experimental import pallas as pl
from jax.experimental.pallas import tpu as pltpu
from jax.sharding import PartitionSpec as P

Q_HEADS = 96
KV_HEADS = 8
NEGATIVE = -1e30
STEP = 512
TILE = 2
AHEAD = 3
KERNEL_VMEM = 24 * 1024 * 1024
STAT_ROWS = 16
META_ROWS = 16

VMEM = pl.BlockSpec(memory_space=pltpu.VMEM)
SMEM = pl.BlockSpec(memory_space=pltpu.SMEM)
HBM = pl.BlockSpec(memory_space=pltpu.HBM)


def prepare_kernel(
    fill_ref,
    place_hbm,
    pos_hbm,
    q_hbm,
    k_hbm,
    v_hbm,
    tk_hbm,
    tv_hbm,
    spread_ref,
    kv_ref,
    bias_ref,
    place_ref,
    pos_ref,
    q_ref,
    k_ref,
    v_ref,
    turn_ref,
    sems,
):
    slots, width = k_ref.shape
    turn = tk_hbm.shape[0]
    pairs = (
        (place_hbm, place_ref),
        (pos_hbm, pos_ref),
        (k_hbm, k_ref),
        (v_hbm, v_ref),
        (q_hbm, q_ref),
        (tk_hbm, turn_ref.at[0]),
        (tv_hbm, turn_ref.at[1]),
    )
    moves = [pltpu.make_async_copy(src, dst, sems.at[n]) for n, (src, dst) in enumerate(pairs)]
    for move in moves:
        move.start()
    ctx = lax.axis_index("ctx")
    sub = lax.axis_index("head") % (lax.axis_size("head") // KV_HEADS)
    core = sub % 2
    moves[0].wait()
    lane = lax.broadcasted_iota(jnp.int32, (1, width), 1)
    seat = jnp.full((1, width), 1 << 20, jnp.int32)
    for n, (at, flip) in enumerate(((ctx, 0), (ctx, 1), (ctx ^ core, 2), (ctx ^ 1 ^ core, 3))):
        for i in range(turn):
            seat = jnp.where(lane == n * turn + i, place_ref[(sub ^ flip) * width + at * turn + i], seat)
    seat = seat.astype(jnp.float32)
    moves[1].wait()
    pos = pos_ref[...].astype(jnp.float32)
    for b in range(pos.shape[0]):
        tokens = jnp.broadcast_to(pos[b : b + 1, :], (width, width)).T
        bias_ref[b * width : (b + 1) * width, :] = jnp.where(seat <= tokens, 0.0, NEGATIVE).astype(jnp.bfloat16)
    fill = jnp.broadcast_to(fill_ref[...], (width, width))
    moves[2].wait()
    first = jnp.broadcast_to(k_ref[0:1, :].astype(jnp.float32), (width, width))
    row = lax.broadcasted_iota(jnp.int32, (width, width), 0)
    for at in range(0, slots, width):
        keys = jnp.where(row + at < fill, k_ref[at : at + width, :].astype(jnp.float32), first)
        kv_ref[at : at + width, :] = keys.T.astype(jnp.bfloat16)
    moves[3].wait()
    for at in range(0, slots, width):
        values = jnp.where(row + at < fill, v_ref[at : at + width, :].astype(jnp.float32), 0.0)
        kv_ref[slots + at : slots + at + width, :] = values.astype(jnp.bfloat16)
    moves[4].wait()
    tokens, columns = q_ref.shape
    for h in range(columns // width):
        own_q = q_ref[:, h * width : (h + 1) * width]
        for at in range(spread_ref.shape[0]):
            spread_ref[at, h * tokens : (h + 1) * tokens, :] = own_q
    moves[5].wait()
    moves[6].wait()
    at = 2 * slots
    kv_ref[at : at + 2 * turn, :] = jnp.concatenate([turn_ref[0], turn_ref[1]], axis=0)
    at += 2 * turn
    half = lax.broadcasted_iota(jnp.int32, (META_ROWS, width), 0) < META_ROWS // 2
    meta = jnp.where(half, fill[:META_ROWS] >> 5, fill[:META_ROWS] & 31)
    kv_ref[at : at + META_ROWS, :] = meta.astype(jnp.float32).astype(jnp.bfloat16)


def attend_kernel(
    q_ref, own_ref, near_ref, far_ref, diagonal_ref, bias_ref, out_ref, total_ref, peak_ref, *, slots, turn
):
    sources = (own_ref, near_ref, far_ref, diagonal_ref)
    blocks, rows, width = q_ref.shape
    tokens = bias_ref.shape[0] // blocks
    heads = rows // tokens
    size = TILE * rows
    tiles = blocks // TILE
    count = turn * len(sources)
    factor = math.log2(math.e) / math.sqrt(width)
    plain = (((1,), (0,)), ((), ()))
    contract = (((1,), (1,)), ((), ()))

    def dot(first, second, dims=plain):
        return lax.dot_general(first, second, dims, preferred_element_type=jnp.float32)

    def weights(scores, peak):
        return jnp.exp2(scores * factor - peak).astype(jnp.bfloat16)

    def visible(source, start):
        meta = source[2 * slots + 2 * turn :, :].astype(jnp.float32)
        half = META_ROWS // 2
        fill = meta[0:1] * 32 + meta[half : half + 1]
        slot = lax.broadcasted_iota(jnp.int32, (STEP, width), 0) + start
        return jnp.where(slot.astype(jnp.float32) < fill, 1.0, 0.0).astype(jnp.bfloat16)

    def turned(index):
        pairs = [s[2 * slots : 2 * slots + 2 * turn, :] for s in sources]
        return jnp.concatenate([p[index * turn : (index + 1) * turn] for p in pairs], axis=0)

    turn_k = turned(0)
    turn_v = jnp.concatenate([turned(1), jnp.ones((count, width), jnp.bfloat16)], axis=1)

    row = lax.broadcasted_iota(jnp.int32, (rows, width), 0)
    lane = lax.broadcasted_iota(jnp.int32, (rows, width), 1)
    stat_row = lax.broadcasted_iota(jnp.int32, (STAT_ROWS, width), 0)

    def finish(t, total, peak):
        for n in range(TILE):
            at = t * TILE + n
            part = total[n * rows : (n + 1) * rows]
            norm = part[:, width:]
            out_ref[at, 0:rows, :] = (part[:, :width] / norm).astype(jnp.bfloat16)
            lse = peak[n * rows : (n + 1) * rows] + jnp.log2(norm)
            flat = jnp.sum(jnp.where(row == lane, lse, 0.0), axis=0, keepdims=True)
            high = flat.astype(jnp.bfloat16).astype(jnp.float32)
            middle = (flat - high).astype(jnp.bfloat16).astype(jnp.float32)
            low = flat - high - middle
            stat = jnp.where(
                stat_row == 0, high, jnp.where(stat_row == 1, middle, jnp.where(stat_row == 2, low, 0.0))
            )
            out_ref[at, rows : rows + STAT_ROWS, :] = stat.astype(jnp.bfloat16)

    def step(start, taken, first, last):
        keys = jnp.concatenate(
            [s[start + b : start + b + width, :] for s in taken for b in range(0, STEP, width)], axis=1
        )
        values = jnp.concatenate(
            [
                jnp.concatenate([s[slots + start : slots + start + STEP, :], visible(s, start)], axis=1)
                for s in taken
            ],
            axis=0,
        )

        def score(t):
            q = jnp.concatenate([q_ref[t * TILE + n] for n in range(TILE)], axis=0)
            if not first:
                return dot(q, keys), None
            bias = jnp.concatenate(
                [
                    bias_ref[(t * TILE + n) * tokens : (t * TILE + n + 1) * tokens, :].astype(jnp.float32)[:, 0:count]
                    for n in range(TILE)
                    for h in range(heads)
                ],
                axis=0,
            )
            return dot(q, keys), dot(q, turn_k, contract) + bias

        def mix(t, scores, fresh):
            at = slice(t * size, (t + 1) * size)
            peak = jnp.max(scores, axis=1, keepdims=True)
            if first:
                peak = jnp.maximum(peak, jnp.max(fresh, axis=1, keepdims=True)) * factor
                total = dot(weights(scores, peak), values) + dot(weights(fresh, peak), turn_v)
            else:
                before = peak_ref[at, 0:1]
                peak = jnp.maximum(before, peak * factor)
                total = total_ref[at, :] * jnp.exp2(before - peak) + dot(weights(scores, peak), values)
            if last:
                finish(t, total, peak)
            else:
                total_ref[at, :] = total
                peak_ref[at, :] = jnp.broadcast_to(peak, (size, width))

        ahead = []
        for t in range(tiles):
            ahead.append((t, *score(t)))
            if len(ahead) > AHEAD:
                mix(*ahead.pop(0))
        for waiting in ahead:
            mix(*waiting)

    def more(source):
        meta = source[2 * slots + 2 * turn :, :].astype(jnp.float32)
        half = META_ROWS // 2
        return jnp.max(meta[:half]) * 32 + jnp.max(meta[half:]) > STEP

    wide = [more(s) for s in (own_ref, far_ref, diagonal_ref)]
    step(0, sources, True, False)

    for mine, first, second in ((0, 0, 0), (0, 0, 1), (0, 1, 0), (1, 0, 1), (1, 1, 0), (1, 1, 1)):
        rest = sources[:2] * mine + sources[2:3] * first + sources[3:] * second
        given = [w if want else jnp.logical_not(w) for w, want in zip(wide, (mine, first, second))]

        @pl.when(given[0] & given[1] & given[2])
        def _(rest=rest):
            if rest:
                step(STEP, rest, False, True)
            else:
                for t in range(tiles):
                    at = slice(t * size, (t + 1) * size)
                    finish(t, total_ref[at, :], peak_ref[at, :])


def combine_kernel(part_ref, out_ref):
    blocks, _, width = part_ref.shape
    tokens, columns = out_ref.shape
    heads = columns // width
    rows = heads * tokens
    pieces = [part_ref[c, rows : rows + STAT_ROWS, :].astype(jnp.float32) for c in range(blocks)]
    lse = jnp.concatenate([p[0:1] + p[1:2] + p[2:3] for p in pieces], axis=0)
    share = jnp.exp2(lse - jnp.max(lse, axis=0, keepdims=True))
    share = share / jnp.sum(share, axis=0, keepdims=True)
    share = jnp.concatenate([share, jnp.zeros((width - blocks, width), jnp.float32)], axis=0).T
    total = jnp.zeros((rows, width), jnp.float32)
    for c in range(blocks):
        total = total + part_ref[c, 0:rows, :].astype(jnp.float32) * share[0:rows, c : c + 1]
    total = total.astype(jnp.bfloat16)
    for h in range(heads):
        out_ref[:, h * width : (h + 1) * width] = total[h * tokens : (h + 1) * tokens]


def prepare(fill, positions, queries, keys, values, turn_k, turn_v, copies):
    slots, width = keys.shape
    seats = (positions.shape[0] // width, width)
    turn = turn_k.shape[0]
    return pl.pallas_call(
        prepare_kernel,
        out_shape=[
            jax.ShapeDtypeStruct((copies, queries.size // width, width), jnp.bfloat16),
            jax.ShapeDtypeStruct((2 * slots + 2 * turn + META_ROWS, width), jnp.bfloat16),
            jax.ShapeDtypeStruct((positions.shape[0], width), jnp.bfloat16),
        ],
        in_specs=[VMEM] + [HBM] * 7,
        out_specs=[VMEM] * 3,
        scratch_shapes=[
            pltpu.SMEM(positions.shape, jnp.int32),
            pltpu.VMEM(seats, jnp.int32),
            pltpu.VMEM(queries.shape, jnp.bfloat16),
            pltpu.VMEM(keys.shape, jnp.bfloat16),
            pltpu.VMEM(values.shape, jnp.bfloat16),
            pltpu.VMEM((2, turn, width), jnp.bfloat16),
            pltpu.SemaphoreType.DMA((7,)),
        ],
        compiler_params=pltpu.CompilerParams(vmem_limit_bytes=56 * 1024 * 1024),
        name="prepare",
    )(fill.reshape(1, 1), positions, positions.reshape(seats), queries, keys, values, turn_k, turn_v)


def attend(q, sources, bias, slots, turn):
    blocks, rows, width = q.shape
    work = blocks * rows * slots * len(sources)
    return pl.pallas_call(
        functools.partial(attend_kernel, slots=slots, turn=turn),
        out_shape=jax.ShapeDtypeStruct((blocks, rows + STAT_ROWS, width), jnp.bfloat16),
        in_specs=[VMEM] * 6,
        out_specs=VMEM,
        scratch_shapes=[
            pltpu.VMEM((blocks * rows, 2 * width), jnp.float32),
            pltpu.VMEM((blocks * rows, width), jnp.float32),
        ],
        compiler_params=pltpu.CompilerParams(vmem_limit_bytes=KERNEL_VMEM),
        cost_estimate=pl.CostEstimate(flops=4 * work * width, bytes_accessed=4 << 20, transcendentals=work),
        name="attend",
    )(q, *sources, bias)


def combine(parts, tokens, columns):
    return pl.pallas_call(
        combine_kernel,
        out_shape=jax.ShapeDtypeStruct((tokens, columns), jnp.bfloat16),
        in_specs=[VMEM],
        out_specs=VMEM,
        compiler_params=pltpu.CompilerParams(vmem_limit_bytes=4 * 1024 * 1024),
        name="combine",
    )(parts)


def body(queries, cache_keys, cache_values, turn_keys, turn_values, cache_fill, turn_positions):
    tokens, columns = queries.shape
    width = cache_keys.shape[2]
    slots = cache_keys.shape[1]
    turn = turn_keys.shape[1]
    n_ctx, n_head = lax.axis_size("ctx"), lax.axis_size("head")
    other = [(h, h ^ 1) for h in range(n_head)]
    across = [
        (c * n_head + h, (c ^ (h & 1)) * n_head + (h ^ 2)) for c in range(n_ctx) for h in range(n_head)
    ]

    copies, own, bias = prepare(
        cache_fill, turn_positions, queries, cache_keys[0], cache_values[0], turn_keys[0], turn_values[0], n_ctx
    )
    q = lax.all_to_all(copies, "ctx", split_axis=0, concat_axis=0, tiled=True)
    far = lax.ppermute(own, ("ctx", "head"), across)
    near = lax.ppermute(own, "head", other)
    diagonal = lax.ppermute(far, "head", other)
    parts = attend(q, (own, near, far, diagonal), bias, slots, turn)
    parts = lax.all_to_all(parts, "ctx", split_axis=0, concat_axis=0, tiled=True)
    return combine(parts, tokens, columns)


def solution(mesh):
    in_specs = (
        P("ctx", "head"),
        P("head", "ctx", None),
        P("head", "ctx", None),
        P("head", "ctx", None),
        P("head", "ctx", None),
        P("ctx"),
        P(),
    )
    return jax.shard_map(body, mesh=mesh, in_specs=in_specs, out_specs=P("ctx", "head"), check_vma=False)
```
